128 devices in a mesh: row: 8 (over z, x_lo), col: 16 (over x_hi, y, core).
Axes of the slice: x: 4 (x_hi: 2, x_lo: 2; x = x_hi * 2 + x_lo), y: 4, z: 4, core: 2. Of those that a mesh axis runs over, the one named last changes fastest.
Arguments:
- amplitudes: bfloat16 [2048, 8, 4096], P('col', None, 'row'), may hold values from -6 to 6
- integrals: bfloat16 [32, 4096, 4096], P(None, 'row', 'col'), may hold values from -0.046875 to 0.046875
- blocks: int32 [32, 2], replicated, may hold values from 0 to 7, as said below
Outputs:
- ladder: bfloat16 [2048, 8, 4096], P(('row', 'col'))
The draws below stay inside these ranges and needn't reach their ends.
Inputs may be any that keep to these rules, and one draw needn't show every extreme that they name: No (contracted tile, output tile) pair appears twice; each of the 8 contracted tiles and each output tile appears in exactly 4 blocks.
All inputs are finite; a program needn't handle non-finite values.
Results may differ from the reference program's by a relative error of at most 0.001.
Values may be sent and summed in bfloat16 or wider, within the bound.
No kernel may reach another device: no remote copies, remote signals or barrier semaphores. Data moves between devices by JAX's collectives and lax.ppermute only.
A program may use at most 192 MiB of HBM per device.

```python
import jax
import jax.numpy as jnp
from jax import lax

PAIR_WIDTH = 4096
PAIR_TILES = 8
BLOCKS = 32
BLK_PER_Q = 4
PAIRS = 2048


def draw_blocks(key, part):
    key_rows, key_cols, key_shuffle = jax.random.split(jax.random.fold_in(key, 17), 3)
    row_perm = jax.random.permutation(key_rows, PAIR_TILES)
    col_perm = jax.random.permutation(key_cols, PAIR_TILES)
    lanes = jnp.arange(BLOCKS) % PAIR_TILES
    turns = jnp.arange(BLOCKS) // PAIR_TILES
    table = jnp.stack([row_perm[lanes], col_perm[(lanes + turns) % PAIR_TILES]], axis=1)
    shuffle = jax.random.permutation(key_shuffle, BLOCKS)
    return table[shuffle].astype(jnp.int32)


def block_levels(stream_key, dims, cuts, least, top_value):
    def one(position, shards_of):
        draws = jax.random.uniform(jax.random.fold_in(jax.random.fold_in(stream_key, 6), position), (shards_of,), jnp.float32, least / len(cuts), top_value / len(cuts))
        return jnp.repeat(jnp.exp(draws), dims[position] // shards_of).reshape((-1,) + (1,) * (len(dims) - position - 1))

    level = one(*cuts[0])
    for cut in cuts[1:]:
        level = level * one(*cut)
    return level


def normal_values(key, extent, deviation, bound, shards=(), held_as=jnp.bfloat16):
    gain = block_levels(key, extent, shards, -0.22, 0.18) if shards else 1.0
    array = jax.random.normal(key, extent, jnp.float32) * deviation * gain
    return jnp.minimum(jnp.maximum(array, -bound), bound).astype(held_as)


def setup_inputs(seed: int = 0) -> dict:
    arg_keys = jax.random.split(jax.random.key(seed), 4)
    return {
        "amplitudes": normal_values(arg_keys[0], (PAIRS, PAIR_TILES, PAIR_WIDTH), 1.0, 6.0, ((0, 16), (2, 8))),
        "integrals": normal_values(arg_keys[1], (BLOCKS, PAIR_WIDTH, PAIR_WIDTH), (BLK_PER_Q * PAIR_WIDTH) ** -0.5, 0.046875, ((1, 8), (2, 16))),
        "blocks": draw_blocks(jax.random.fold_in(arg_keys[3], 71), 0),
    }


def reference(amplitudes, integrals, blocks):
    running = jnp.zeros((PAIRS, PAIR_TILES, PAIR_WIDTH), jnp.float32)

    def add_block(which_block, running):
        row_tile = blocks[which_block, 0].astype(jnp.int32)
        col_tile = blocks[which_block, 1].astype(jnp.int32)
        left_rows = lax.dynamic_index_in_dim(amplitudes, row_tile, 1, keepdims=False).astype(jnp.float32)
        right_cols = lax.dynamic_index_in_dim(integrals, which_block, 0, keepdims=False).astype(jnp.float32)
        product = jnp.dot(left_rows, right_cols, preferred_element_type=jnp.float32)
        current = lax.dynamic_index_in_dim(running, col_tile, 1, keepdims=False)
        return lax.dynamic_update_index_in_dim(running, current + product, col_tile, 1)

    running = lax.fori_loop(jnp.int32(0), jnp.int32(BLOCKS), add_block, running)
    return running.astype(jnp.bfloat16)
```

```python
import functools

import jax
import jax.numpy as jnp
from jax import lax
from jax.experimental import pallas as pl
from jax.experimental.pallas import tpu as pltpu
from jax.sharding import PartitionSpec as P

PIECES = 4
STEP = 256.0
TOP = 32700.0
TAIL = 16


def table(target):
    pairs = []
    for z in range(4):
        for xl in range(2):
            for xh in range(2):
                for y in range(4):
                    for k in range(2):
                        src = (z * 2 + xl) * 16 + xh * 8 + y * 2 + k
                        z2, xl2, xh2, y2, k2 = target(z, xl, xh, y, k)
                        dst = ((z2 % 4) * 2 + xl2) * 16 + xh2 * 8 + (y2 % 4) * 2 + k2
                        pairs.append((src, dst))
    return pairs


def way(k):
    return 1 - 2 * k


CORE = table(lambda z, xl, xh, y, k: (z, xl, xh, y, 1 - k))
X_HI = table(lambda z, xl, xh, y, k: (z, xl, 1 - xh, y, k))
Y_FORE = table(lambda z, xl, xh, y, k: (z, xl, xh, y + way(k), k))
Y_BACK = table(lambda z, xl, xh, y, k: (z, xl, xh, y - way(k), k))
Z_FORE = table(lambda z, xl, xh, y, k: (z + way(k), xl, xh, y, k))
Z_BACK = table(lambda z, xl, xh, y, k: (z - way(k), xl, xh, y, k))
X_SAME = table(lambda z, xl, xh, y, k: (z, xl, k, y, xh))
X_OTHER = table(lambda z, xl, xh, y, k: (z, 1 - xl, k, y, xh))
GROUPS = [list(range(8)), list(range(8, 16))]


def move(array, pairs):
    return lax.ppermute(array, ("row", "col"), pairs)


def encode(values):
    top = jnp.max(jnp.abs(values), axis=0, keepdims=True)
    code = jnp.ceil(jnp.log2(jnp.maximum(top, 1e-30)) * STEP) + 1.0
    scaled = jnp.round(values * (jnp.exp2(code * (-1.0 / STEP)) * TOP))
    return scaled.astype(jnp.int32).astype(jnp.int16), code


def scales(message_ref):
    rows = message_ref.shape[0]
    codes = message_ref[rows - TAIL :, :].astype(jnp.int32).astype(jnp.float32)
    return jnp.exp2(codes * (1.0 / STEP)) * (1.0 / TOP)


def decode(message_ref, scale, group, rows):
    held = message_ref[group * rows : (group + 1) * rows, :]
    return held.astype(jnp.int32).astype(jnp.float32) * scale[group : group + 1, :]


def put_codes(message_ref, codes):
    rows, width = message_ref.shape
    codes = codes + [jnp.zeros((1, width), jnp.float32)] * (TAIL - len(codes))
    block = jnp.concatenate(codes, axis=0)
    message_ref[rows - TAIL :, :] = block.astype(jnp.int32).astype(jnp.int16)


def partial_kernel(blk, prow, pos, a0, a1, a2, a3, *rest):
    v_own, v_other = rest[0:4], rest[4:8]
    far_ref, back_ref, own_ref, next_ref, held, far_codes, back_codes = rest[8:]
    q = pl.program_id(0)
    rows = a0.shape[2]
    width = held.shape[2]
    half = width // 2
    for part, v in enumerate((v_own, v_other)):
        total = None
        for j in range(4):
            tile = prow[q * 4 + j]
            left = jnp.concatenate([a[s, tile] for a in (a0, a1, a2, a3) for s in range(2)], axis=0)
            term = jnp.dot(left, v[j][0], preferred_element_type=jnp.float32)
            total = term if total is None else total + term
        for s in range(8):
            held[pos[s], :, part * half : (part + 1) * half] = total[s * rows : (s + 1) * rows]
    own_ref[...] = held[0:2]
    next_ref[...] = held[2:4]
    for g in range(2):
        at = pl.ds(pl.multiple_of((q * 2 + g) * rows, rows), rows)
        for ref, codes, slot in ((far_ref, far_codes, 4), (back_ref, back_codes, 6)):
            message, code = encode(held[slot + g])
            ref[at, :] = message
            codes[pl.ds(q * 2 + g, 1), :] = code

    @pl.when(q == pl.num_programs(0) - 1)
    def _():
        for ref, codes in ((far_ref, far_codes), (back_ref, back_codes)):
            last = ref.shape[0] - TAIL
            ref[last:, :] = codes[...].astype(jnp.int32).astype(jnp.int16)


def relay_kernel(next_ref, came_ref, out_ref):
    groups, rows, _ = next_ref.shape
    scale = scales(came_ref)
    codes = []
    for g in range(groups):
        total = next_ref[g] + decode(came_ref, scale, g, rows)
        out_ref[g * rows : (g + 1) * rows, :], code = encode(total)
        codes.append(code)
    put_codes(out_ref, codes)


def gather_kernel(own_ref, came_ref, back_ref, same_ref, other_ref):
    groups, rows, _ = own_ref.shape
    came_scale, back_scale = scales(came_ref), scales(back_ref)
    codes = ([], [])
    for g in range(groups):
        total = own_ref[g] + decode(came_ref, came_scale, g, rows) + decode(back_ref, back_scale, g, rows)
        message, code = encode(total)
        at = g // 2
        (same_ref, other_ref)[g % 2][at * rows : (at + 1) * rows, :] = message
        codes[g % 2].append(code)
    put_codes(same_ref, codes[0])
    put_codes(other_ref, codes[1])


def finish_kernel(swap, same_ref, other_ref, out_ref):
    tiles, rows, width = out_ref.shape
    half = width // 2
    same_scale, other_scale = scales(same_ref), scales(other_ref)
    for q in range(tiles):
        total = decode(same_ref, same_scale, q, rows) + decode(other_ref, other_scale, q, rows)
        turned = jnp.concatenate([total[:, half:], total[:, :half]], axis=1)
        out_ref[q] = jnp.where(swap[0] == 1, turned, total).astype(out_ref.dtype)


LIMIT = 48 * 2**20


def partial(blk, prow, pos, gathered, v_own, v_other):
    _, tiles, rows, depth = gathered[0].shape
    half = v_own.shape[2]
    width = 2 * half
    groups = 2 * tiles

    def whole(shape):
        return pl.BlockSpec(shape, lambda q, *_: (0,) * len(shape))

    def block(j):
        return pl.BlockSpec((1, depth, half), lambda q, blk, prow, pos, j=j: (blk[q * 4 + j], 0, 0))

    message = jax.ShapeDtypeStruct((groups * rows + TAIL, width), jnp.int16)
    kept = jax.ShapeDtypeStruct((groups, rows, width), jnp.float32)
    flops = 2 * 8 * rows * 4 * depth * width * tiles
    return pl.pallas_call(
        partial_kernel,
        grid_spec=pltpu.PrefetchScalarGridSpec(
            num_scalar_prefetch=3,
            grid=(tiles,),
            in_specs=[whole(gathered[0].shape)] * 4 + [block(j) for j in range(4)] * 2,
            out_specs=[whole(message.shape)] * 2 + [pl.BlockSpec((2, rows, width), lambda q, *_: (q, 0, 0))] * 2,
            scratch_shapes=[
                pltpu.VMEM((8, rows, width), jnp.float32),
                pltpu.VMEM((TAIL, width), jnp.float32),
                pltpu.VMEM((TAIL, width), jnp.float32),
            ],
        ),
        out_shape=[message, message, kept, kept],
        compiler_params=pltpu.CompilerParams(vmem_limit_bytes=LIMIT),
        cost_estimate=pl.CostEstimate(flops=flops, bytes_accessed=24 * 2**20, transcendentals=0),
        name="partial",
    )(blk, prow, pos, *gathered, *[v_own] * 4, *[v_other] * 4)


def simple(kernel, outs, args, name, scalars=0):
    vmem = pl.BlockSpec(memory_space=pltpu.VMEM)
    smem = pl.BlockSpec(memory_space=pltpu.SMEM)
    return pl.pallas_call(
        kernel,
        out_shape=outs,
        in_specs=[smem] * scalars + [vmem] * (len(args) - scalars),
        out_specs=jax.tree.map(lambda _: vmem, outs),
        compiler_params=pltpu.CompilerParams(vmem_limit_bytes=LIMIT),
        cost_estimate=pl.CostEstimate(flops=2**22, bytes_accessed=2**22, transcendentals=0),
        name=name,
    )(*args)


def on_device(amplitudes, integrals, blocks):
    pairs, tiles, depth = amplitudes.shape
    half = integrals.shape[2]
    width = 2 * half
    per = pairs // 8 // PIECES
    rows = 8 * per
    row, col = lax.axis_index("row"), lax.axis_index("col")
    z, x_lo = row // 2, row % 2
    x_hi, y, core = col // 8, (col // 2) % 4, col % 2
    turn = 1 - 2 * core

    key = blocks[:, 1] * 32 + jnp.arange(32, dtype=jnp.int32)
    rank = jnp.sum((key[None, :] < key[:, None]).astype(jnp.int32), axis=1)
    hit = (rank[None, :] == jnp.arange(32, dtype=jnp.int32)[:, None]).astype(jnp.int32)
    blk = jnp.sum(hit * jnp.arange(32, dtype=jnp.int32)[None, :], axis=1)
    prow = jnp.sum(hit * blocks[:, 0][None, :], axis=1)

    slots = []
    for shift in (0, -turn, turn, 2):
        for flip in (0, 1):
            from_y = (y + shift + 4) % 4
            from_x = x_hi ^ flip
            to_z = 2 * from_x + from_y // 2
            ahead = ((to_z - z) * turn + 8) % 4
            slots.append(ahead * 2 + ((from_y % 2) ^ x_lo))
    pos = jnp.stack(slots).astype(jnp.int32)
    swap = x_hi.astype(jnp.int32).reshape(1)

    shards = amplitudes.reshape(8, PIECES, per, tiles, depth).transpose(1, 3, 0, 2, 4)
    shards = shards.reshape(PIECES, 1, tiles, rows, depth)
    v_other = move(integrals, CORE)

    message = jax.ShapeDtypeStruct((2 * tiles * rows + TAIL, width), jnp.int16)
    small = jax.ShapeDtypeStruct((tiles * rows + TAIL, width), jnp.int16)
    outs = []
    for p in range(PIECES):
        own = shards[p]
        a0 = jnp.concatenate([own, move(own, X_HI)], axis=0)
        a1 = move(a0, Y_FORE)
        a2 = move(a0, Y_BACK)
        a3 = move(a1, Y_FORE)
        far, back, kept, nxt = partial(blk, prow, pos, (a0, a1, a2, a3), integrals, v_other)
        came = move(far, Z_FORE)
        back = move(back, Z_BACK)
        relayed = simple(relay_kernel, message, (nxt, came), "relay")
        came = move(relayed, Z_FORE)
        same, other = simple(gather_kernel, [small, small], (kept, came, back), "collect")
        same = move(same, X_SAME)
        other = move(other, X_OTHER)
        done = simple(
            finish_kernel,
            jax.ShapeDtypeStruct((tiles, rows, width), jnp.bfloat16),
            (swap, same, other),
            "finish",
            scalars=1,
        )
        outs.append(done.reshape(tiles, 8, per, width))
    done = jnp.stack(outs, axis=2).reshape(tiles, 8, PIECES * per, width).transpose(1, 2, 0, 3)
    done = lax.all_to_all(done, "col", 0, 0, axis_index_groups=GROUPS, tiled=True)
    done = done.reshape(4, 2, PIECES * per, tiles, width).transpose(2, 3, 1, 0, 4)
    return done.reshape(PIECES * per, tiles, 8 * width)


def solution(mesh):
    return jax.shard_map(
        on_device,
        mesh=mesh,
        in_specs=(P("col", None, "row"), P(None, "row", "col"), P()),
        out_specs=P(("row", "col"), None, None),
        check_vma=False,
    )
```

```python
import functools

import jax
import jax.numpy as jnp
from jax import lax
from jax.experimental import pallas as pl
from jax.experimental.pallas import tpu as pltpu
from jax.sharding import PartitionSpec as P

PIECES = (4, 4, 4, 4)
ORDER = (
    ("stage", 0),
    ("join", 1),
    ("multiply", 0),
    ("forward", 1),
    ("join", 2),
    ("multiply", 1),
    ("forward", 2),
    ("join", 3),
    ("relay", 0),
    ("multiply", 2),
    ("forward", 3),
    ("relay", 1),
    ("multiply", 3),
    ("collect", (0, 1)),
    ("relay", 2),
    ("finish", (0, 1)),
    ("relay", 3),
    ("collect", (2, 3)),
    ("finish", (2, 3)),
)
STEP = 256.0
TOP = 32700.0


def tail(groups):
    return (groups + 15) // 16 * 16


def table(target):
    pairs = []
    for z in range(4):
        for xl in range(2):
            for xh in range(2):
                for y in range(4):
                    for k in range(2):
                        src = (z * 2 + xl) * 16 + xh * 8 + y * 2 + k
                        z2, xl2, xh2, y2, k2 = target(z, xl, xh, y, k)
                        dst = ((z2 % 4) * 2 + xl2) * 16 + xh2 * 8 + (y2 % 4) * 2 + k2
                        pairs.append((src, dst))
    return pairs


def way(k):
    return 1 - 2 * k


CORE = table(lambda z, xl, xh, y, k: (z, xl, xh, y, 1 - k))
X_HI = table(lambda z, xl, xh, y, k: (z, xl, 1 - xh, y, k))
Y_FORE = table(lambda z, xl, xh, y, k: (z, xl, xh, y + way(k), k))
Y_BACK = table(lambda z, xl, xh, y, k: (z, xl, xh, y - way(k), k))
Z_FORE = table(lambda z, xl, xh, y, k: (z + way(k), xl, xh, y, k))
Z_BACK = table(lambda z, xl, xh, y, k: (z - way(k), xl, xh, y, k))
X_SAME = [table(lambda z, xl, xh, y, k, b=b: (z, xl, k, y, xh ^ b)) for b in range(2)]
X_OTHER = [table(lambda z, xl, xh, y, k, b=b: (z, 1 - xl, k, y, xh ^ b)) for b in range(2)]
Y_SHIFT = [table(lambda z, xl, xh, y, k, a=a: (z, xl, xh, y + a, k)) for a in range(4)]


def move(array, pairs):
    return lax.ppermute(array, ("row", "col"), pairs)


def encode(values):
    top = jnp.max(jnp.abs(values), axis=0, keepdims=True)
    code = jnp.ceil(jnp.log2(jnp.maximum(top, 1e-30)) * STEP) + 1.0
    scaled = jnp.round(values * (jnp.exp2(code * (-1.0 / STEP)) * TOP))
    return scaled.astype(jnp.int32).astype(jnp.int16), code


def scales(message_ref, groups):
    codes = message_ref[message_ref.shape[0] - tail(groups) :, :]
    return jnp.exp2(codes.astype(jnp.int32).astype(jnp.float32) * (1.0 / STEP)) * (1.0 / TOP)


def decode(message_ref, scale, group, start, rows):
    held = message_ref[start : start + rows, :]
    return held.astype(jnp.int32).astype(jnp.float32) * scale[group : group + 1, :]


def put_codes(message_ref, codes):
    rows, width = message_ref.shape
    more = tail(len(codes)) - len(codes)
    block = jnp.concatenate(codes + [jnp.zeros((1, width), jnp.float32)] * more, axis=0)
    message_ref[rows - tail(len(codes)) :, :] = block.astype(jnp.int32).astype(jnp.int16)


def stage_kernel(where, own_ref, came_ref, *rest):
    out_ref, sems = rest[-2:]
    half = own_ref.shape[2]
    core = where[2]
    copies = []
    for n, (ref, side) in enumerate(((own_ref, core), (came_ref, 1 - core))):
        at = pl.ds(pl.multiple_of(side * half, half), half)
        copies.append(pltpu.make_async_copy(ref, out_ref.at[:, :, at], sems.at[n]))
    for copy in copies:
        copy.start()
    for copy in copies:
        copy.wait()


def partial_kernel(blk, prow, pos, a0, a1, a2, a3, v_ref, *rest):
    far_ref, back_ref, own_ref, next_ref, held, far_codes, back_codes = rest[-7:]
    q = pl.program_id(0)
    rows = a0.shape[2]
    total = None
    for j in range(4):
        tile = prow[q * 4 + j]
        left = jnp.concatenate([a[s, tile] for a in (a0, a1, a2, a3) for s in range(2)], axis=0)
        term = jnp.dot(left, v_ref[blk[q * 4 + j]], preferred_element_type=jnp.float32)
        total = term if total is None else total + term
    for s in range(8):
        held[pos[s]] = total[s * rows : (s + 1) * rows]
    own_ref[...] = held[0:2]
    next_ref[...] = held[2:4]
    for g in range(2):
        at = pl.ds(pl.multiple_of((q * 2 + g) * rows, rows), rows)
        for ref, codes, slot in ((far_ref, far_codes, 4), (back_ref, back_codes, 6)):
            message, code = encode(held[slot + g])
            ref[at, :] = message
            codes[pl.ds(q * 2 + g, 1), :] = code

    @pl.when(q == pl.num_programs(0) - 1)
    def _():
        for ref, codes in ((far_ref, far_codes), (back_ref, back_codes)):
            last = ref.shape[0] - codes.shape[0]
            ref[last:, :] = codes[...].astype(jnp.int32).astype(jnp.int16)


def join_kernel(own_ref, came_ref, *rest):
    rest[-1][0] = own_ref[0]
    rest[-1][1] = came_ref[0]


def copy_kernel(in_ref, *rest):
    rest[-1][...] = in_ref[...]


def relay_kernel(next_ref, came_ref, *rest):
    out_ref = rest[-1]
    groups, rows, _ = next_ref.shape
    scale = scales(came_ref, groups)
    codes = []
    for g in range(groups):
        total = next_ref[g] + decode(came_ref, scale, g, g * rows, rows)
        out_ref[g * rows : (g + 1) * rows, :], code = encode(total)
        codes.append(code)
    put_codes(out_ref, codes)


def collect_kernel(count, x_hi, *refs):
    pieces, outs = [refs[3 * i : 3 * i + 3] for i in range(count)], refs[-4:]
    codes, at, flip = ([], []), 0, x_hi[0] == 1
    for own_ref, came_ref, back_ref in pieces:
        groups, rows, _ = own_ref.shape
        came_scale, back_scale = scales(came_ref, groups), scales(back_ref, groups)
        half = rows // 2
        for g in range(groups):
            total = own_ref[g] + decode(came_ref, came_scale, g, g * rows, rows)
            total = total + decode(back_ref, back_scale, g, g * rows, rows)
            message, code = encode(total)
            first, second = message[:half].astype(jnp.int32), message[half:].astype(jnp.int32)
            near = slice(at, at + half)
            outs[2 * (g % 2)][near, :] = jnp.where(flip, second, first).astype(jnp.int16)
            outs[2 * (g % 2) + 1][near, :] = jnp.where(flip, first, second).astype(jnp.int16)
            codes[g % 2].append(code)
            at += half * (g % 2)
    for k in range(4):
        put_codes(outs[k], codes[k // 2])


def finish_kernel(pers, where, *refs):
    sums, out_ref = refs[:4], refs[-1]
    y, core = where[1], where[2]
    _, _, tiles, width2 = out_ref.shape
    width = width2 // 2
    groups = tiles * len(pers)
    scale = [scales(ref, groups) for ref in sums]
    start = base = 0
    for n, per in enumerate(pers):
        rows = 4 * per
        parts = []
        for b in range(2):
            stack = []
            for q in range(tiles):
                g, near = n * tiles + q, start + q * rows
                total = decode(sums[b], scale[b], g, near, rows) + decode(sums[2 + b], scale[2 + b], g, near, rows)
                stack.append(total)
            parts.append(jnp.swapaxes(jnp.stack(stack, axis=0), 0, 1))
        first = jnp.where(core == 0, parts[0], parts[1]).astype(out_ref.dtype)
        second = jnp.where(core == 0, parts[1], parts[0]).astype(out_ref.dtype)
        for to_y in range(4):
            slot = lax.rem(to_y - y + 4, 4)
            out_ref[slot, base : base + per, :, :width] = first[to_y * per : (to_y + 1) * per]
            out_ref[slot, base : base + per, :, width:] = second[to_y * per : (to_y + 1) * per]
        start += tiles * rows
        base += per


def place_kernel(count, where, *refs):
    parts, out_ref = refs[:count], refs[-1]
    base = 0
    for n in range(0, len(parts), 4):
        per = parts[n].shape[0]
        width = parts[n].shape[-1] // 2
        for a in range(4):
            from_y = lax.rem(where[1] - a + 4, 4)
            held = parts[n + a][...]
            for x in range(2):
                at = pl.ds(pl.multiple_of((x * 4 + from_y) * width, width), width)
                out_ref[base : base + per, :, at] = held[:, :, x * width : (x + 1) * width]
        base += per


LIMIT = 14 * 2**20


def stage(where, own, came):
    blocks, depth, half = own.shape
    return pl.pallas_call(
        stage_kernel,
        out_shape=pltpu.VMEM((blocks, depth, 2 * half), own.dtype),
        in_specs=[pl.BlockSpec(memory_space=pltpu.SMEM)] + [pl.BlockSpec(memory_space=pl.ANY)] * 2,
        out_specs=pl.BlockSpec(memory_space=pltpu.VMEM),
        scratch_shapes=[pltpu.SemaphoreType.DMA((2,))],
        compiler_params=pltpu.CompilerParams(vmem_limit_bytes=LIMIT),
        cost_estimate=pl.CostEstimate(flops=0, bytes_accessed=16 * 2**20, transcendentals=0),
        name="stage",
    )(where, pltpu.with_memory_space_constraint(own, pltpu.HBM), pltpu.with_memory_space_constraint(came, pltpu.HBM))


def partial(blk, prow, pos, gathered, staged):
    _, tiles, rows, depth = gathered[0].shape
    width = staged.shape[2]
    groups = 2 * tiles

    def whole(shape):
        return pl.BlockSpec(shape, lambda q, *_: (0,) * len(shape))

    message = jax.ShapeDtypeStruct((groups * rows + tail(groups), width), jnp.int16)
    kept = jax.ShapeDtypeStruct((groups, rows, width), jnp.float32)
    flops = 2 * 8 * rows * 4 * depth * width * tiles
    return pl.pallas_call(
        partial_kernel,
        grid_spec=pltpu.PrefetchScalarGridSpec(
            num_scalar_prefetch=3,
            grid=(tiles,),
            in_specs=[whole(gathered[0].shape)] * 4
            + [pl.BlockSpec(memory_space=pltpu.VMEM)],
            out_specs=[whole(message.shape)] * 2 + [pl.BlockSpec((2, rows, width), lambda q, *_: (q, 0, 0))] * 2,
            scratch_shapes=[
                pltpu.VMEM((8, rows, width), jnp.float32),
                pltpu.VMEM((tail(groups), width), jnp.float32),
                pltpu.VMEM((tail(groups), width), jnp.float32),
            ],
        ),
        out_shape=[message, message, kept, kept],
        compiler_params=pltpu.CompilerParams(vmem_limit_bytes=LIMIT),
        cost_estimate=pl.CostEstimate(flops=flops, bytes_accessed=24 * 2**20, transcendentals=0),
        name="partial",
    )(blk, prow, pos, *gathered, pltpu.with_memory_space_constraint(staged, pltpu.VMEM))


def simple(kernel, outs, args, name, scalars=0):
    vmem = pl.BlockSpec(memory_space=pltpu.VMEM)
    smem = pl.BlockSpec(memory_space=pltpu.SMEM)
    return pl.pallas_call(
        kernel,
        out_shape=outs,
        in_specs=[smem] * scalars + [vmem] * (len(args) - scalars),
        out_specs=jax.tree.map(lambda _: vmem, outs),
        compiler_params=pltpu.CompilerParams(vmem_limit_bytes=LIMIT),
        cost_estimate=pl.CostEstimate(flops=2**22, bytes_accessed=2**22, transcendentals=0),
        name=name,
    )(*args)


def later(array, *others):
    return lax.optimization_barrier((array, *others))[0]


def on_device(amplitudes, integrals, blocks):
    _, tiles, depth = amplitudes.shape
    width = 2 * integrals.shape[2]
    row, col = lax.axis_index("row"), lax.axis_index("col")
    z, x_lo = row // 2, row % 2
    x_hi, y, core = col // 8, (col // 2) % 4, col % 2
    turn = 1 - 2 * core
    where = jnp.stack([x_hi, y, core]).astype(jnp.int32)

    number = jnp.arange(32, dtype=jnp.int32)
    key = blocks[:, 1] * 32 + number
    rank = jnp.sum((key[None, :] < key[:, None]).astype(jnp.int32), axis=1)
    hit = (rank[None, :] == number[:, None]).astype(jnp.int32)
    blk = jnp.sum(hit * number[None, :], axis=1)
    prow = jnp.sum(hit * blocks[:, 0][None, :], axis=1)

    slots = []
    for shift in (0, -turn, turn, 2):
        for flip in (0, 1):
            from_y = (y + shift + 4) % 4
            from_x = x_hi ^ flip
            to_z = 2 * from_x + from_y // 2
            ahead = ((to_z - z) * turn + 8) % 4
            slots.append(ahead * 2 + ((from_y % 2) ^ x_lo))
    pos = jnp.stack(slots).astype(jnp.int32)

    last = []

    def run(kernel, outs, args, name, scalars=0, after=()):
        args = list(args)
        args[scalars] = later(args[scalars], *last[-1:], *after)
        out = simple(kernel, outs, args, name, scalars)
        last.append(jax.tree.leaves(out)[0])
        return out

    shards = amplitudes.reshape(4, 2, 16, tiles, depth).transpose(3, 1, 0, 2, 4)
    first = PIECES[0]
    own = [shards[:, :, :, :first].reshape(1, tiles, 8 * first, depth)]
    came = [move(own[0], X_HI)]
    v_other = move(integrals, CORE)
    at, rest = first, []
    for per in PIECES[1:]:
        rest.append(shards[:, :, :, at : at + per].reshape(1, tiles, 8 * per, depth))
        at += per
    own += rest
    gathered = []

    def join(p):
        per = PIECES[p]
        shape = jax.ShapeDtypeStruct((2, tiles, 8 * per, depth), jnp.bfloat16)
        before = gathered[-1][1:3] if gathered else ()
        a0 = run(join_kernel, shape, (own[p], came[p]), "join", after=before)
        a1, a2 = move(a0, Y_FORE), move(a0, Y_BACK)
        gathered.append([a0, a1, a2, None])

    def forward(p):
        a1 = later(gathered[p][1], last[-1])
        gathered[p][3] = move(a1, Y_FORE)

    sums, ends, placed, staged = [], {}, [], []

    def multiply(p):
        a0, a1, a2, a3 = gathered[p]
        far, back, kept, nxt = partial(blk, prow, pos, (later(a0, last[-1]), a1, a2, a3), staged[0])
        last.append(far)
        sums.append((kept, nxt, move(far, Z_FORE), move(back, Z_BACK)))

    def relay(p):
        kept, nxt, far, back = sums[p]
        message = jax.ShapeDtypeStruct((16 * 8 * PIECES[p] + 16, width), jnp.int16)
        out = run(relay_kernel, message, (nxt, far), "relay", after=(back,))
        ends[p] = (kept, move(out, Z_FORE), back)

    def collect(members):
        groups = tiles * len(members)
        rows = tiles * 4 * sum(PIECES[p] for p in members)
        small = jax.ShapeDtypeStruct((rows + tail(groups), width), jnp.int16)
        args = [array for p in members for array in ends[p]]
        kernel = functools.partial(collect_kernel, len(members))
        out = run(kernel, [small] * 4, (where[:1], *args), "collect", scalars=1)
        return [move(m, t) for m, t in zip(out, X_SAME + X_OTHER)]

    def finish(members, out):
        pers = tuple(PIECES[p] for p in members)
        shape = jax.ShapeDtypeStruct((4, sum(pers), tiles, 2 * width), jnp.bfloat16)
        done = run(functools.partial(finish_kernel, pers), shape, (where, *out), "finish", scalars=1)
        placed.extend([done[0]] + [move(done[a], Y_SHIFT[a]) for a in range(1, 4)])

    join(0)
    forward(0)
    moved = run(copy_kernel, jax.ShapeDtypeStruct((1, tiles, 8 * (16 - first), depth), jnp.bfloat16),
                (jnp.concatenate(rest, axis=2),), "rest")
    moved = move(moved, X_HI)
    at = 0
    for per in PIECES[1:]:
        came.append(moved[:, :, at : at + 8 * per])
        at += 8 * per
    pending = {}
    for step in ORDER:
        name, p = step[0], step[1]
        if name == "join":
            join(p)
        elif name == "stage":
            staged.append(stage(later(where, last[-1]), integrals, v_other))
        elif name == "forward":
            forward(p)
        elif name == "multiply":
            multiply(p)
        elif name == "relay":
            relay(p)
        elif name == "collect":
            pending[p] = collect(p)
        else:
            finish(p, pending[p])
    return simple(
        functools.partial(place_kernel, len(placed)),
        jax.ShapeDtypeStruct((16, tiles, 8 * width), jnp.bfloat16),
        (where, *placed),
        "place",
        scalars=1,
    )


def solution(mesh):
    return jax.shard_map(
        on_device,
        mesh=mesh,
        in_specs=(P("col", None, "row"), P(None, "row", "col"), P()),
        out_specs=P(("row", "col"), None, None),
        check_vma=False,
    )
```

```python
import functools

import jax
import jax.numpy as jnp
from jax import lax
from jax.experimental import pallas as pl
from jax.experimental.pallas import tpu as pltpu
from jax.sharding import PartitionSpec as P

PIECES = (4, 4, 4, 4)
ORDER = (
    ("join", 1),
    ("fetch", (2, 3)),
    ("turn", 0),
    ("stage", 0),
    ("forward", 1),
    ("join", 2),
    ("multiply", 1),
    ("forward", 2),
    ("join", 3),
    ("multiply", 0),
    ("relay", 1),
    ("relay", 0),
    ("multiply", 2),
    ("forward", 3),
    ("collect", (0, 1)),
    ("multiply", 3),
    ("relay", 2),
    ("finish", (0, 1)),
    ("relay", 3),
    ("collect", (2, 3)),
    ("finish", (2, 3)),
)
STEP = 256.0
TOP = 32700.0


def tail(groups):
    return (groups + 15) // 16 * 16


def table(target):
    pairs = []
    for z in range(4):
        for xl in range(2):
            for xh in range(2):
                for y in range(4):
                    for k in range(2):
                        src = (z * 2 + xl) * 16 + xh * 8 + y * 2 + k
                        z2, xl2, xh2, y2, k2 = target(z, xl, xh, y, k)
                        dst = ((z2 % 4) * 2 + xl2) * 16 + xh2 * 8 + (y2 % 4) * 2 + k2
                        pairs.append((src, dst))
    return pairs


def way(k):
    return 1 - 2 * k


CORE = table(lambda z, xl, xh, y, k: (z, xl, xh, y, 1 - k))
X_HI = table(lambda z, xl, xh, y, k: (z, xl, 1 - xh, y, k))
Y_FORE = table(lambda z, xl, xh, y, k: (z, xl, xh, y + way(k), k))
Y_BACK = table(lambda z, xl, xh, y, k: (z, xl, xh, y - way(k), k))
Z_FORE = table(lambda z, xl, xh, y, k: (z + way(k), xl, xh, y, k))
Z_BACK = table(lambda z, xl, xh, y, k: (z - way(k), xl, xh, y, k))
X_SAME = [table(lambda z, xl, xh, y, k, b=b: (z, xl, k, y, xh ^ b)) for b in range(2)]
X_OTHER = [table(lambda z, xl, xh, y, k, b=b: (z, 1 - xl, k, y, xh ^ b)) for b in range(2)]
Y_SHIFT = [table(lambda z, xl, xh, y, k, a=a: (z, xl, xh, y + a, k)) for a in range(4)]


def move(array, pairs):
    return lax.ppermute(array, ("row", "col"), pairs)


def encode(values):
    top = jnp.max(jnp.abs(values), axis=0, keepdims=True)
    code = jnp.ceil(jnp.log2(jnp.maximum(top, 1e-30)) * STEP) + 1.0
    scaled = jnp.round(values * (jnp.exp2(code * (-1.0 / STEP)) * TOP))
    return scaled.astype(jnp.int32).astype(jnp.int16), code


def scales(message_ref, groups):
    codes = message_ref[message_ref.shape[0] - tail(groups) :, :]
    return jnp.exp2(codes.astype(jnp.int32).astype(jnp.float32) * (1.0 / STEP)) * (1.0 / TOP)


def decode(message_ref, scale, group, start, rows):
    held = message_ref[start : start + rows, :]
    return held.astype(jnp.int32).astype(jnp.float32) * scale[group : group + 1, :]


def put_codes(message_ref, codes):
    rows, width = message_ref.shape
    more = tail(len(codes)) - len(codes)
    block = jnp.concatenate(codes + [jnp.zeros((1, width), jnp.float32)] * more, axis=0)
    message_ref[rows - tail(len(codes)) :, :] = block.astype(jnp.int32).astype(jnp.int16)


def stage_kernel(where, own_ref, came_ref, *rest):
    out_ref, sems = rest[-2:]
    half = own_ref.shape[2]
    core = where[2]
    copies = []
    for n, (ref, side) in enumerate(((own_ref, core), (came_ref, 1 - core))):
        at = pl.ds(pl.multiple_of(side * half, half), half)
        copies.append(pltpu.make_async_copy(ref, out_ref.at[:, :, at], sems.at[n]))
    for copy in copies:
        copy.start()
    for copy in copies:
        copy.wait()


def partial_kernel(blk, prow, pos, *rest):
    far_ref, back_ref, own_ref, next_ref, held, far_codes, back_codes = rest[-7:]
    *shards, v_ref = rest[:-7]
    q = pl.program_id(0)
    rows = shards[0].shape[2]
    total = None
    for j in range(4):
        tile = prow[q * 4 + j]
        left = jnp.concatenate([a[s, tile] for a in shards for s in range(a.shape[0])], axis=0)
        term = jnp.dot(left, v_ref[blk[q * 4 + j]], preferred_element_type=jnp.float32)
        total = term if total is None else total + term
    for s in range(8):
        held[pos[s]] = total[s * rows : (s + 1) * rows]
    own_ref[...] = held[0:2]
    next_ref[...] = held[2:4]
    for g in range(2):
        at = pl.ds(pl.multiple_of((q * 2 + g) * rows, rows), rows)
        for ref, codes, slot in ((far_ref, far_codes, 4), (back_ref, back_codes, 6)):
            message, code = encode(held[slot + g])
            ref[at, :] = message
            codes[pl.ds(q * 2 + g, 1), :] = code

    @pl.when(q == pl.num_programs(0) - 1)
    def _():
        for ref, codes in ((far_ref, far_codes), (back_ref, back_codes)):
            last = ref.shape[0] - codes.shape[0]
            ref[last:, :] = codes[...].astype(jnp.int32).astype(jnp.int16)


def join_kernel(*refs):
    for n, ref in enumerate(refs[:-1]):
        refs[-1][n] = ref[0]


def copy_kernel(in_ref, *rest):
    rest[-1][...] = in_ref[...]


def relay_kernel(next_ref, came_ref, *rest):
    out_ref = rest[-1]
    groups, rows, _ = next_ref.shape
    scale = scales(came_ref, groups)
    codes = []
    for g in range(groups):
        total = next_ref[g] + decode(came_ref, scale, g, g * rows, rows)
        out_ref[g * rows : (g + 1) * rows, :], code = encode(total)
        codes.append(code)
    put_codes(out_ref, codes)


def collect_kernel(count, x_hi, *refs):
    pieces, outs = [refs[3 * i : 3 * i + 3] for i in range(count)], refs[-4:]
    codes, at, flip = ([], []), 0, x_hi[0] == 1
    for own_ref, came_ref, back_ref in pieces:
        groups, rows, _ = own_ref.shape
        came_scale, back_scale = scales(came_ref, groups), scales(back_ref, groups)
        half = rows // 2
        for g in range(groups):
            total = own_ref[g] + decode(came_ref, came_scale, g, g * rows, rows)
            total = total + decode(back_ref, back_scale, g, g * rows, rows)
            message, code = encode(total)
            first, second = message[:half].astype(jnp.int32), message[half:].astype(jnp.int32)
            near = slice(at, at + half)
            outs[2 * (g % 2)][near, :] = jnp.where(flip, second, first).astype(jnp.int16)
            outs[2 * (g % 2) + 1][near, :] = jnp.where(flip, first, second).astype(jnp.int16)
            codes[g % 2].append(code)
            at += half * (g % 2)
    for k in range(4):
        put_codes(outs[k], codes[k // 2])


def finish_kernel(pers, where, *refs):
    sums, out_ref = refs[:4], refs[-1]
    y, core = where[1], where[2]
    _, _, tiles, width2 = out_ref.shape
    width = width2 // 2
    groups = tiles * len(pers)
    scale = [scales(ref, groups) for ref in sums]
    start = base = 0
    for n, per in enumerate(pers):
        rows = 4 * per
        parts = []
        for b in range(2):
            stack = []
            for q in range(tiles):
                g, near = n * tiles + q, start + q * rows
                total = decode(sums[b], scale[b], g, near, rows) + decode(sums[2 + b], scale[2 + b], g, near, rows)
                stack.append(total)
            parts.append(jnp.swapaxes(jnp.stack(stack, axis=0), 0, 1))
        first = jnp.where(core == 0, parts[0], parts[1]).astype(out_ref.dtype)
        second = jnp.where(core == 0, parts[1], parts[0]).astype(out_ref.dtype)
        for to_y in range(4):
            slot = lax.rem(to_y - y + 4, 4)
            out_ref[slot, base : base + per, :, :width] = first[to_y * per : (to_y + 1) * per]
            out_ref[slot, base : base + per, :, width:] = second[to_y * per : (to_y + 1) * per]
        start += tiles * rows
        base += per


def place_kernel(count, where, *refs):
    parts, out_ref = refs[:count], refs[-1]
    base = 0
    for n in range(0, len(parts), 4):
        per = parts[n].shape[0]
        width = parts[n].shape[-1] // 2
        for a in range(4):
            from_y = lax.rem(where[1] - a + 4, 4)
            held = parts[n + a][...]
            for x in range(2):
                at = pl.ds(pl.multiple_of((x * 4 + from_y) * width, width), width)
                out_ref[base : base + per, :, at] = held[:, :, x * width : (x + 1) * width]
        base += per


LIMIT = 10 * 2**20


def stage(where, own, came):
    blocks, depth, half = own.shape
    return pl.pallas_call(
        stage_kernel,
        out_shape=pltpu.VMEM((blocks, depth, 2 * half), own.dtype),
        in_specs=[pl.BlockSpec(memory_space=pltpu.SMEM)] + [pl.BlockSpec(memory_space=pl.ANY)] * 2,
        out_specs=pl.BlockSpec(memory_space=pltpu.VMEM),
        scratch_shapes=[pltpu.SemaphoreType.DMA((2,))],
        compiler_params=pltpu.CompilerParams(vmem_limit_bytes=LIMIT),
        cost_estimate=pl.CostEstimate(flops=0, bytes_accessed=16 * 2**20, transcendentals=0),
        name="stage",
    )(where, pltpu.with_memory_space_constraint(own, pltpu.HBM), pltpu.with_memory_space_constraint(came, pltpu.HBM))


def partial(blk, prow, pos, gathered, staged):
    _, tiles, rows, depth = gathered[0].shape
    width = staged.shape[2]
    groups = 2 * tiles

    def whole(shape):
        return pl.BlockSpec(shape, lambda q, *_: (0,) * len(shape))

    message = jax.ShapeDtypeStruct((groups * rows + tail(groups), width), jnp.int16)
    kept = pltpu.HBM((groups, rows, width), jnp.float32)
    flops = 2 * 8 * rows * 4 * depth * width * tiles
    return pl.pallas_call(
        partial_kernel,
        grid_spec=pltpu.PrefetchScalarGridSpec(
            num_scalar_prefetch=3,
            grid=(tiles,),
            in_specs=[whole(a.shape) for a in gathered]
            + [pl.BlockSpec(memory_space=pltpu.VMEM)],
            out_specs=[whole(message.shape)] * 2 + [pl.BlockSpec((2, rows, width), lambda q, *_: (q, 0, 0))] * 2,
            scratch_shapes=[
                pltpu.VMEM((8, rows, width), jnp.float32),
                pltpu.VMEM((tail(groups), width), jnp.float32),
                pltpu.VMEM((tail(groups), width), jnp.float32),
            ],
        ),
        out_shape=[message, message, kept, kept],
        compiler_params=pltpu.CompilerParams(vmem_limit_bytes=LIMIT),
        cost_estimate=pl.CostEstimate(flops=flops, bytes_accessed=24 * 2**20, transcendentals=0),
        name="partial",
    )(blk, prow, pos, *gathered, pltpu.with_memory_space_constraint(staged, pltpu.VMEM))


def simple(kernel, outs, args, name, scalars=0):
    vmem = pl.BlockSpec(memory_space=pltpu.VMEM)
    smem = pl.BlockSpec(memory_space=pltpu.SMEM)
    return pl.pallas_call(
        kernel,
        out_shape=outs,
        in_specs=[smem] * scalars + [vmem] * (len(args) - scalars),
        out_specs=jax.tree.map(lambda _: vmem, outs),
        compiler_params=pltpu.CompilerParams(vmem_limit_bytes=LIMIT),
        cost_estimate=pl.CostEstimate(flops=2**22, bytes_accessed=2**22, transcendentals=0),
        name=name,
    )(*args)


def later(array, *others):
    return lax.optimization_barrier((array, *others))[0]


def on_device(amplitudes, integrals, blocks):
    _, tiles, depth = amplitudes.shape
    width = 2 * integrals.shape[2]
    row, col = lax.axis_index("row"), lax.axis_index("col")
    z, x_lo = row // 2, row % 2
    x_hi, y, core = col // 8, (col // 2) % 4, col % 2
    turn = 1 - 2 * core
    where = jnp.stack([x_hi, y, core]).astype(jnp.int32)

    number = jnp.arange(32, dtype=jnp.int32)
    key = blocks[:, 1] * 32 + number
    rank = jnp.sum((key[None, :] < key[:, None]).astype(jnp.int32), axis=1)
    hit = (rank[None, :] == number[:, None]).astype(jnp.int32)
    blk = jnp.sum(hit * number[None, :], axis=1)
    prow = jnp.sum(hit * blocks[:, 0][None, :], axis=1)

    slots = []
    for shift in (0, -turn, turn, 2):
        for flip in (0, 1):
            from_y = (y + shift + 4) % 4
            from_x = x_hi ^ flip
            to_z = 2 * from_x + from_y // 2
            ahead = ((to_z - z) * turn + 8) % 4
            slots.append(ahead * 2 + ((from_y % 2) ^ x_lo))
    pos = jnp.stack(slots).astype(jnp.int32)
    pos_first = jnp.stack(slots[0::2] + slots[1::2]).astype(jnp.int32)

    last = []

    def run(kernel, outs, args, name, scalars=0, after=()):
        args = list(args)
        args[scalars] = later(args[scalars], *last[-1:], *after)
        out = simple(kernel, outs, args, name, scalars)
        last.append(jax.tree.leaves(out)[0])
        return out

    shards = amplitudes.reshape(4, 2, 16, tiles, depth).transpose(3, 1, 0, 2, 4)
    own, at = [], 0
    for per in PIECES:
        own.append(shards[:, :, :, at : at + per].reshape(1, tiles, 8 * per, depth))
        at += per
    came = {1: move(own[1], X_HI)}
    v_other = move(integrals, CORE)
    gathered = {}

    def send(p, a0):
        gathered[p] = [a0, move(a0, Y_FORE), move(a0, Y_BACK), None]

    def forward(p):
        a1 = later(gathered[p][1], *last[-1:])
        gathered[p][3] = move(a1, Y_FORE)

    def fetch(members):
        rows = [8 * PIECES[p] for p in members]
        shape = jax.ShapeDtypeStruct((1, tiles, sum(rows), depth), jnp.bfloat16)
        block = jnp.concatenate([own[p] for p in members], axis=2)
        moved = move(run(copy_kernel, shape, (block,), "rest", after=(came[1],)), X_HI)
        at = 0
        for p, n in zip(members, rows):
            came[p] = moved[:, :, at : at + n]
            at += n

    def join(p):
        shape = jax.ShapeDtypeStruct((2, tiles, 8 * PIECES[p], depth), jnp.bfloat16)
        send(p, run(join_kernel, shape, (own[p], came[p]), "join", after=gathered[p - 1][1:3]))

    def turn_first():
        shape = jax.ShapeDtypeStruct((4, tiles, 8 * PIECES[0], depth), jnp.bfloat16)
        held = run(join_kernel, shape, tuple(gathered[0]), "join")
        gathered[0] = (held, move(held, X_HI))

    sums, ends, placed, staged = {}, {}, [], []

    def multiply(p):
        held = (later(gathered[p][0], last[-1]), *gathered[p][1:])
        far, back, kept, nxt = partial(blk, prow, pos if p else pos_first, held, staged[0])
        last.append(far)
        sums[p] = (kept, nxt, move(far, Z_FORE), move(back, Z_BACK))

    def relay(p):
        kept, nxt, far, back = sums[p]
        message = jax.ShapeDtypeStruct((16 * 8 * PIECES[p] + 16, width), jnp.int16)
        out = run(relay_kernel, message, (nxt, far), "relay", after=(back,))
        ends[p] = (kept, move(out, Z_FORE), back)

    def collect(members):
        groups = tiles * len(members)
        rows = tiles * 4 * sum(PIECES[p] for p in members)
        small = jax.ShapeDtypeStruct((rows + tail(groups), width), jnp.int16)
        args = [array for p in members for array in ends[p]]
        kernel = functools.partial(collect_kernel, len(members))
        out = run(kernel, [small] * 4, (where[:1], *args), "collect", scalars=1)
        return [move(m, t) for m, t in zip(out, X_SAME + X_OTHER)]

    def finish(members, out):
        pers = tuple(PIECES[p] for p in members)
        shape = jax.ShapeDtypeStruct((4, sum(pers), tiles, 2 * width), jnp.bfloat16)
        done = run(functools.partial(finish_kernel, pers), shape, (where, *out), "finish", scalars=1)
        placed.extend([done[0]] + [move(done[a], Y_SHIFT[a]) for a in range(1, 4)])

    send(0, own[0])
    forward(0)
    pending = {}
    for step in ORDER:
        name, p = step[0], step[1]
        if name == "join":
            join(p)
        elif name == "stage":
            staged.append(stage(later(where, last[-1]), integrals, v_other))
        elif name == "forward":
            forward(p)
        elif name == "fetch":
            fetch(p)
        elif name == "turn":
            turn_first()
        elif name == "multiply":
            multiply(p)
        elif name == "relay":
            relay(p)
        elif name == "collect":
            pending[p] = collect(p)
        else:
            finish(p, pending[p])
    return simple(
        functools.partial(place_kernel, len(placed)),
        jax.ShapeDtypeStruct((16, tiles, 8 * width), jnp.bfloat16),
        (where, *placed),
        "place",
        scalars=1,
    )


def solution(mesh):
    return jax.shard_map(
        on_device,
        mesh=mesh,
        in_specs=(P("col", None, "row"), P(None, "row", "col"), P()),
        out_specs=P(("row", "col"), None, None),
        check_vma=False,
    )
```

```python
import functools

import jax
import jax.numpy as jnp
from jax import lax
from jax.experimental import pallas as pl
from jax.experimental.pallas import tpu as pltpu
from jax.sharding import PartitionSpec as P

PIECES = (4, 4, 4, 4)
ORDER = (
    ("join", 1),
    ("fetch", (2, 3)),
    ("turn", 0),
    ("stage", 0),
    ("forward", 1),
    ("join", 2),
    ("multiply", 1),
    ("forward", 2),
    ("join", 3),
    ("multiply", 0),
    ("relay", 1),
    ("relay", 0),
    ("forward", 3),
    ("multiply", 2),
    ("collect", (0, 1)),
    ("multiply", 3),
    ("relay", 2),
    ("finish", (0, 1)),
    ("relay", 3),
    ("collect", (2, 3)),
    ("finish", (2, 3)),
)
STEP = 256.0
TOP = 32700.0


def tail(groups):
    return (groups + 15) // 16 * 16


def table(target):
    pairs = []
    for z in range(4):
        for xl in range(2):
            for xh in range(2):
                for y in range(4):
                    for k in range(2):
                        src = (z * 2 + xl) * 16 + xh * 8 + y * 2 + k
                        z2, xl2, xh2, y2, k2 = target(z, xl, xh, y, k)
                        dst = ((z2 % 4) * 2 + xl2) * 16 + xh2 * 8 + (y2 % 4) * 2 + k2
                        pairs.append((src, dst))
    return pairs


def way(k):
    return 1 - 2 * k


CORE = table(lambda z, xl, xh, y, k: (z, xl, xh, y, 1 - k))
X_HI = table(lambda z, xl, xh, y, k: (z, xl, 1 - xh, y, k))
Y_FORE = table(lambda z, xl, xh, y, k: (z, xl, xh, y + way(k), k))
Y_BACK = table(lambda z, xl, xh, y, k: (z, xl, xh, y - way(k), k))
Z_FORE = table(lambda z, xl, xh, y, k: (z + way(k), xl, xh, y, k))
Z_BACK = table(lambda z, xl, xh, y, k: (z - way(k), xl, xh, y, k))
X_SAME = [table(lambda z, xl, xh, y, k, b=b: (z, xl, k, y, xh ^ b)) for b in range(2)]
X_OTHER = [table(lambda z, xl, xh, y, k, b=b: (z, 1 - xl, k, y, xh ^ b)) for b in range(2)]
Y_SHIFT = [table(lambda z, xl, xh, y, k, a=a: (z, xl, xh, y + a, k)) for a in range(4)]


def move(array, pairs):
    return lax.ppermute(array, ("row", "col"), pairs)


def encode(values):
    top = jnp.max(jnp.abs(values), axis=0, keepdims=True)
    code = jnp.ceil(jnp.log2(jnp.maximum(top, 1e-30)) * STEP) + 1.0
    scaled = jnp.round(values * (jnp.exp2(code * (-1.0 / STEP)) * TOP))
    return scaled.astype(jnp.int32).astype(jnp.int16), code


def scales(message_ref, groups):
    codes = message_ref[message_ref.shape[0] - tail(groups) :, :]
    return jnp.exp2(codes.astype(jnp.int32).astype(jnp.float32) * (1.0 / STEP)) * (1.0 / TOP)


def decode(message_ref, scale, group, start, rows):
    held = message_ref[start : start + rows, :]
    return held.astype(jnp.int32).astype(jnp.float32) * scale[group : group + 1, :]


def put_codes(message_ref, codes):
    rows, width = message_ref.shape
    more = tail(len(codes)) - len(codes)
    block = jnp.concatenate(codes + [jnp.zeros((1, width), jnp.float32)] * more, axis=0)
    message_ref[rows - tail(len(codes)) :, :] = block.astype(jnp.int32).astype(jnp.int16)


def stage_kernel(where, own_ref, came_ref, *rest):
    out_ref, sems = rest[-2:]
    half = own_ref.shape[2]
    core = where[2]
    copies = []
    for n, (ref, side) in enumerate(((own_ref, core), (came_ref, 1 - core))):
        at = pl.ds(pl.multiple_of(side * half, half), half)
        copies.append(pltpu.make_async_copy(ref, out_ref.at[:, :, at], sems.at[n]))
    for copy in copies:
        copy.start()
    for copy in copies:
        copy.wait()


def partial_kernel(blk, prow, pos, *rest):
    far_ref, back_ref, own_ref, next_ref, held, far_codes, back_codes = rest[-7:]
    *shards, v_ref = rest[:-7]
    q = pl.program_id(0)
    rows = shards[0].shape[2]
    total = None
    for j in range(4):
        tile = prow[q * 4 + j]
        left = jnp.concatenate([a[s, tile] for a in shards for s in range(a.shape[0])], axis=0)
        term = jnp.dot(left, v_ref[blk[q * 4 + j]], preferred_element_type=jnp.float32)
        total = term if total is None else total + term
    for s in range(8):
        held[pos[s]] = total[s * rows : (s + 1) * rows]
    own_ref[...] = held[0:2]
    next_ref[...] = held[2:4]
    for g in range(2):
        at = pl.ds(pl.multiple_of((q * 2 + g) * rows, rows), rows)
        for ref, codes, slot in ((far_ref, far_codes, 4), (back_ref, back_codes, 6)):
            message, code = encode(held[slot + g])
            ref[at, :] = message
            codes[pl.ds(q * 2 + g, 1), :] = code

    @pl.when(q == pl.num_programs(0) - 1)
    def _():
        for ref, codes in ((far_ref, far_codes), (back_ref, back_codes)):
            last = ref.shape[0] - codes.shape[0]
            ref[last:, :] = codes[...].astype(jnp.int32).astype(jnp.int16)


def join_kernel(*refs):
    for n, ref in enumerate(refs[:-1]):
        refs[-1][n] = ref[0]


def copy_kernel(in_ref, *rest):
    rest[-1][...] = in_ref[...]


def relay_kernel(next_ref, came_ref, *rest):
    out_ref = rest[-1]
    groups, rows, _ = next_ref.shape
    scale = scales(came_ref, groups)
    codes = []
    for g in range(groups):
        total = next_ref[g] + decode(came_ref, scale, g, g * rows, rows)
        out_ref[g * rows : (g + 1) * rows, :], code = encode(total)
        codes.append(code)
    put_codes(out_ref, codes)


def collect_kernel(count, x_hi, *refs):
    pieces, outs = [refs[3 * i : 3 * i + 3] for i in range(count)], refs[-4:]
    codes, at, flip = ([], []), 0, x_hi[0] == 1
    for own_ref, came_ref, back_ref in pieces:
        groups, rows, _ = own_ref.shape
        came_scale, back_scale = scales(came_ref, groups), scales(back_ref, groups)
        half = rows // 2
        for g in range(groups):
            total = own_ref[g] + decode(came_ref, came_scale, g, g * rows, rows)
            total = total + decode(back_ref, back_scale, g, g * rows, rows)
            message, code = encode(total)
            first, second = message[:half].astype(jnp.int32), message[half:].astype(jnp.int32)
            near = slice(at, at + half)
            outs[2 * (g % 2)][near, :] = jnp.where(flip, second, first).astype(jnp.int16)
            outs[2 * (g % 2) + 1][near, :] = jnp.where(flip, first, second).astype(jnp.int16)
            codes[g % 2].append(code)
            at += half * (g % 2)
    for k in range(4):
        put_codes(outs[k], codes[k // 2])


def finish_kernel(pers, where, *refs):
    sums, out_ref = refs[:4], refs[-1]
    y, core = where[1], where[2]
    _, _, tiles, width2 = out_ref.shape
    width = width2 // 2
    groups = tiles * len(pers)
    scale = [scales(ref, groups) for ref in sums]
    start = base = 0
    for n, per in enumerate(pers):
        rows = 4 * per
        parts = []
        for b in range(2):
            stack = []
            for q in range(tiles):
                g, near = n * tiles + q, start + q * rows
                total = decode(sums[b], scale[b], g, near, rows) + decode(sums[2 + b], scale[2 + b], g, near, rows)
                stack.append(total)
            parts.append(jnp.swapaxes(jnp.stack(stack, axis=0), 0, 1))
        first = jnp.where(core == 0, parts[0], parts[1]).astype(out_ref.dtype)
        second = jnp.where(core == 0, parts[1], parts[0]).astype(out_ref.dtype)
        for to_y in range(4):
            slot = lax.rem(to_y - y + 4, 4)
            out_ref[slot, base : base + per, :, :width] = first[to_y * per : (to_y + 1) * per]
            out_ref[slot, base : base + per, :, width:] = second[to_y * per : (to_y + 1) * per]
        start += tiles * rows
        base += per


def place_kernel(count, where, *refs):
    parts, out_ref = refs[:count], refs[-1]
    base = 0
    for n in range(0, len(parts), 4):
        per = parts[n].shape[0]
        width = parts[n].shape[-1] // 2
        for a in range(4):
            from_y = lax.rem(where[1] - a + 4, 4)
            held = parts[n + a][...]
            for x in range(2):
                at = pl.ds(pl.multiple_of((x * 4 + from_y) * width, width), width)
                out_ref[base : base + per, :, at] = held[:, :, x * width : (x + 1) * width]
        base += per


LIMIT = 10 * 2**20


def stage(where, own, came):
    blocks, depth, half = own.shape
    return pl.pallas_call(
        stage_kernel,
        out_shape=pltpu.VMEM((blocks, depth, 2 * half), own.dtype),
        in_specs=[pl.BlockSpec(memory_space=pltpu.SMEM)] + [pl.BlockSpec(memory_space=pl.ANY)] * 2,
        out_specs=pl.BlockSpec(memory_space=pltpu.VMEM),
        scratch_shapes=[pltpu.SemaphoreType.DMA((2,))],
        compiler_params=pltpu.CompilerParams(vmem_limit_bytes=LIMIT),
        cost_estimate=pl.CostEstimate(flops=0, bytes_accessed=16 * 2**20, transcendentals=0),
        name="stage",
    )(where, pltpu.with_memory_space_constraint(own, pltpu.HBM), pltpu.with_memory_space_constraint(came, pltpu.HBM))


def partial(blk, prow, pos, gathered, staged):
    _, tiles, rows, depth = gathered[0].shape
    width = staged.shape[2]
    groups = 2 * tiles

    def whole(shape):
        return pl.BlockSpec(shape, lambda q, *_: (0,) * len(shape))

    message = jax.ShapeDtypeStruct((groups * rows + tail(groups), width), jnp.int16)
    kept = jax.ShapeDtypeStruct((groups, rows, width), jnp.float32)
    flops = 2 * 8 * rows * 4 * depth * width * tiles
    return pl.pallas_call(
        partial_kernel,
        grid_spec=pltpu.PrefetchScalarGridSpec(
            num_scalar_prefetch=3,
            grid=(tiles,),
            in_specs=[whole(a.shape) for a in gathered]
            + [pl.BlockSpec(memory_space=pltpu.VMEM)],
            out_specs=[whole(message.shape)] * 2 + [pl.BlockSpec((2, rows, width), lambda q, *_: (q, 0, 0))] * 2,
            scratch_shapes=[
                pltpu.VMEM((8, rows, width), jnp.float32),
                pltpu.VMEM((tail(groups), width), jnp.float32),
                pltpu.VMEM((tail(groups), width), jnp.float32),
            ],
        ),
        out_shape=[message, message, kept, kept],
        compiler_params=pltpu.CompilerParams(vmem_limit_bytes=LIMIT),
        cost_estimate=pl.CostEstimate(flops=flops, bytes_accessed=24 * 2**20, transcendentals=0),
        name="partial",
    )(blk, prow, pos, *gathered, pltpu.with_memory_space_constraint(staged, pltpu.VMEM))


def simple(kernel, outs, args, name, scalars=0):
    vmem = pl.BlockSpec(memory_space=pltpu.VMEM)
    smem = pl.BlockSpec(memory_space=pltpu.SMEM)
    return pl.pallas_call(
        kernel,
        out_shape=outs,
        in_specs=[smem] * scalars + [vmem] * (len(args) - scalars),
        out_specs=jax.tree.map(lambda _: vmem, outs),
        compiler_params=pltpu.CompilerParams(vmem_limit_bytes=LIMIT),
        cost_estimate=pl.CostEstimate(flops=2**22, bytes_accessed=2**22, transcendentals=0),
        name=name,
    )(*args)


def later(array, *others):
    return lax.optimization_barrier((array, *others))[0]


def on_device(amplitudes, integrals, blocks):
    _, tiles, depth = amplitudes.shape
    width = 2 * integrals.shape[2]
    row, col = lax.axis_index("row"), lax.axis_index("col")
    z, x_lo = row // 2, row % 2
    x_hi, y, core = col // 8, (col // 2) % 4, col % 2
    turn = 1 - 2 * core
    where = jnp.stack([x_hi, y, core]).astype(jnp.int32)

    number = jnp.arange(32, dtype=jnp.int32)
    key = blocks[:, 1] * 32 + number
    rank = jnp.sum((key[None, :] < key[:, None]).astype(jnp.int32), axis=1)
    hit = (rank[None, :] == number[:, None]).astype(jnp.int32)
    blk = jnp.sum(hit * number[None, :], axis=1)
    prow = jnp.sum(hit * blocks[:, 0][None, :], axis=1)

    slots = []
    for shift in (0, -turn, turn, 2):
        for flip in (0, 1):
            from_y = (y + shift + 4) % 4
            from_x = x_hi ^ flip
            to_z = 2 * from_x + from_y // 2
            ahead = ((to_z - z) * turn + 8) % 4
            slots.append(ahead * 2 + ((from_y % 2) ^ x_lo))
    pos = jnp.stack(slots).astype(jnp.int32)
    pos_first = jnp.stack(slots[0::2] + slots[1::2]).astype(jnp.int32)

    last = []

    def run(kernel, outs, args, name, scalars=0, after=()):
        args = list(args)
        args[scalars] = later(args[scalars], *last[-1:], *after)
        out = simple(kernel, outs, args, name, scalars)
        last.append(jax.tree.leaves(out)[0])
        return out

    shards = amplitudes.reshape(4, 2, 16, tiles, depth).transpose(3, 1, 0, 2, 4)
    own, at = [], 0
    for per in PIECES:
        own.append(shards[:, :, :, at : at + per].reshape(1, tiles, 8 * per, depth))
        at += per
    came = {1: move(own[1], X_HI)}
    v_other = move(integrals, CORE)
    gathered = {}

    def send(p, a0):
        gathered[p] = [a0, move(a0, Y_FORE), move(a0, Y_BACK), None]

    def forward(p):
        a1 = later(gathered[p][1], *last[-1:])
        gathered[p][3] = move(a1, Y_FORE)

    def fetch(members):
        rows = [8 * PIECES[p] for p in members]
        shape = jax.ShapeDtypeStruct((1, tiles, sum(rows), depth), jnp.bfloat16)
        block = jnp.concatenate([own[p] for p in members], axis=2)
        moved = move(run(copy_kernel, shape, (block,), "rest", after=(came[1],)), X_HI)
        at = 0
        for p, n in zip(members, rows):
            came[p] = moved[:, :, at : at + n]
            at += n

    def join(p):
        shape = jax.ShapeDtypeStruct((2, tiles, 8 * PIECES[p], depth), jnp.bfloat16)
        send(p, run(join_kernel, shape, (own[p], came[p]), "join", after=gathered[p - 1][1:3]))

    def turn_first():
        shape = jax.ShapeDtypeStruct((4, tiles, 8 * PIECES[0], depth), jnp.bfloat16)
        held = run(join_kernel, shape, tuple(gathered[0]), "join")
        gathered[0] = (held, move(held, X_HI))

    sums, ends, placed, staged = {}, {}, [], []

    def multiply(p):
        held = (later(gathered[p][0], last[-1]), *gathered[p][1:])
        far, back, kept, nxt = partial(blk, prow, pos if p else pos_first, held, staged[0])
        last.append(far)
        sums[p] = (kept, nxt, move(far, Z_FORE), move(back, Z_BACK))

    def relay(p):
        kept, nxt, far, back = sums[p]
        message = jax.ShapeDtypeStruct((16 * 8 * PIECES[p] + 16, width), jnp.int16)
        out = run(relay_kernel, message, (nxt, far), "relay", after=(back,))
        ends[p] = (kept, move(out, Z_FORE), back)

    def collect(members):
        groups = tiles * len(members)
        rows = tiles * 4 * sum(PIECES[p] for p in members)
        small = jax.ShapeDtypeStruct((rows + tail(groups), width), jnp.int16)
        args = [array for p in members for array in ends[p]]
        kernel = functools.partial(collect_kernel, len(members))
        out = run(kernel, [small] * 4, (where[:1], *args), "collect", scalars=1)
        return [move(m, t) for m, t in zip(out, X_SAME + X_OTHER)]

    def finish(members, out):
        pers = tuple(PIECES[p] for p in members)
        shape = jax.ShapeDtypeStruct((4, sum(pers), tiles, 2 * width), jnp.bfloat16)
        done = run(functools.partial(finish_kernel, pers), shape, (where, *out), "finish", scalars=1)
        placed.extend([done[0]] + [move(done[a], Y_SHIFT[a]) for a in range(1, 4)])

    send(0, own[0])
    forward(0)
    pending = {}
    for step in ORDER:
        name, p = step[0], step[1]
        if name == "join":
            join(p)
        elif name == "stage":
            staged.append(stage(later(where, last[-1]), integrals, v_other))
        elif name == "forward":
            forward(p)
        elif name == "fetch":
            fetch(p)
        elif name == "turn":
            turn_first()
        elif name == "multiply":
            multiply(p)
        elif name == "relay":
            relay(p)
        elif name == "collect":
            pending[p] = collect(p)
        else:
            finish(p, pending[p])
    return simple(
        functools.partial(place_kernel, len(placed)),
        jax.ShapeDtypeStruct((16, tiles, 8 * width), jnp.bfloat16),
        (where, *placed),
        "place",
        scalars=1,
    )


def solution(mesh):
    return jax.shard_map(
        on_device,
        mesh=mesh,
        in_specs=(P("col", None, "row"), P(None, "row", "col"), P()),
        out_specs=P(("row", "col"), None, None),
        check_vma=False,
    )
```

```python
import functools

import jax
import jax.numpy as jnp
from jax import lax
from jax.experimental import pallas as pl
from jax.experimental.pallas import tpu as pltpu
from jax.sharding import PartitionSpec as P

PIECES = (4, 4, 4, 4)
ORDER = (
    ("join", 1),
    ("fetch", (2, 3)),
    ("turn", 0),
    ("stage", 0),
    ("forward", 1),
    ("join", 2),
    ("multiply", 1),
    ("forward", 2),
    ("join", 3),
    ("multiply", 0),
    ("relay", 1),
    ("forward", 3),
    ("relay", 0),
    ("multiply", 2),
    ("collect", (0, 1)),
    ("multiply", 3),
    ("relay", 2),
    ("finish", (0, 1)),
    ("relay", 3),
    ("collect", (2, 3)),
    ("finish", (2, 3)),
)
STEP = 256.0
TOP = 32700.0


def tail(groups):
    return (groups + 15) // 16 * 16


def table(target):
    pairs = []
    for z in range(4):
        for xl in range(2):
            for xh in range(2):
                for y in range(4):
                    for k in range(2):
                        src = (z * 2 + xl) * 16 + xh * 8 + y * 2 + k
                        z2, xl2, xh2, y2, k2 = target(z, xl, xh, y, k)
                        dst = ((z2 % 4) * 2 + xl2) * 16 + xh2 * 8 + (y2 % 4) * 2 + k2
                        pairs.append((src, dst))
    return pairs


def way(k):
    return 1 - 2 * k


CORE = table(lambda z, xl, xh, y, k: (z, xl, xh, y, 1 - k))
X_HI = table(lambda z, xl, xh, y, k: (z, xl, 1 - xh, y, k))
Y_FORE = table(lambda z, xl, xh, y, k: (z, xl, xh, y + way(k), k))
Y_BACK = table(lambda z, xl, xh, y, k: (z, xl, xh, y - way(k), k))
Z_FORE = table(lambda z, xl, xh, y, k: (z + way(k), xl, xh, y, k))
Z_BACK = table(lambda z, xl, xh, y, k: (z - way(k), xl, xh, y, k))
X_SAME = [table(lambda z, xl, xh, y, k, b=b: (z, xl, k, y, xh ^ b)) for b in range(2)]
X_OTHER = [table(lambda z, xl, xh, y, k, b=b: (z, 1 - xl, k, y, xh ^ b)) for b in range(2)]
Y_SHIFT = [table(lambda z, xl, xh, y, k, a=a: (z, xl, xh, y + a, k)) for a in range(4)]


def move(array, pairs):
    return lax.ppermute(array, ("row", "col"), pairs)


def encode(values):
    top = jnp.max(jnp.abs(values), axis=0, keepdims=True)
    code = jnp.ceil(jnp.log2(jnp.maximum(top, 1e-30)) * STEP) + 1.0
    scaled = jnp.round(values * (jnp.exp2(code * (-1.0 / STEP)) * TOP))
    return scaled.astype(jnp.int32).astype(jnp.int16), code


def scales(message_ref, groups):
    codes = message_ref[message_ref.shape[0] - tail(groups) :, :]
    return jnp.exp2(codes.astype(jnp.int32).astype(jnp.float32) * (1.0 / STEP)) * (1.0 / TOP)


def decode(message_ref, scale, group, start, rows):
    held = message_ref[start : start + rows, :]
    return held.astype(jnp.int32).astype(jnp.float32) * scale[group : group + 1, :]


def put_codes(message_ref, codes):
    rows, width = message_ref.shape
    more = tail(len(codes)) - len(codes)
    block = jnp.concatenate(codes + [jnp.zeros((1, width), jnp.float32)] * more, axis=0)
    message_ref[rows - tail(len(codes)) :, :] = block.astype(jnp.int32).astype(jnp.int16)


def stage_kernel(where, own_ref, came_ref, *rest):
    out_ref, sems = rest[-2:]
    half = own_ref.shape[2]
    core = where[2]
    copies = []
    for n, (ref, side) in enumerate(((own_ref, core), (came_ref, 1 - core))):
        at = pl.ds(pl.multiple_of(side * half, half), half)
        copies.append(pltpu.make_async_copy(ref, out_ref.at[:, :, at], sems.at[n]))
    for copy in copies:
        copy.start()
    for copy in copies:
        copy.wait()


def partial_kernel(blk, prow, pos, *rest):
    far_ref, back_ref, own_ref, next_ref, held, far_codes, back_codes = rest[-7:]
    *shards, v_ref = rest[:-7]
    q = pl.program_id(0)
    rows = shards[0].shape[2]
    total = None
    for j in range(4):
        tile = prow[q * 4 + j]
        left = jnp.concatenate([a[s, tile] for a in shards for s in range(a.shape[0])], axis=0)
        term = jnp.dot(left, v_ref[blk[q * 4 + j]], preferred_element_type=jnp.float32)
        total = term if total is None else total + term
    for s in range(8):
        held[pos[s]] = total[s * rows : (s + 1) * rows]
    own_ref[...] = held[0:2]
    next_ref[...] = held[2:4]
    for g in range(2):
        at = pl.ds(pl.multiple_of((q * 2 + g) * rows, rows), rows)
        for ref, codes, slot in ((far_ref, far_codes, 4), (back_ref, back_codes, 6)):
            message, code = encode(held[slot + g])
            ref[at, :] = message
            codes[pl.ds(q * 2 + g, 1), :] = code

    @pl.when(q == pl.num_programs(0) - 1)
    def _():
        for ref, codes in ((far_ref, far_codes), (back_ref, back_codes)):
            last = ref.shape[0] - codes.shape[0]
            ref[last:, :] = codes[...].astype(jnp.int32).astype(jnp.int16)


def join_kernel(*refs):
    for n, ref in enumerate(refs[:-1]):
        refs[-1][n] = ref[0]


def copy_kernel(in_ref, *rest):
    rest[-1][...] = in_ref[...]


def relay_kernel(next_ref, came_ref, *rest):
    out_ref = rest[-1]
    groups, rows, _ = next_ref.shape
    scale = scales(came_ref, groups)
    codes = []
    for g in range(groups):
        total = next_ref[g] + decode(came_ref, scale, g, g * rows, rows)
        out_ref[g * rows : (g + 1) * rows, :], code = encode(total)
        codes.append(code)
    put_codes(out_ref, codes)


def collect_kernel(count, x_hi, *refs):
    pieces, outs = [refs[3 * i : 3 * i + 3] for i in range(count)], refs[-4:]
    codes, at, flip = ([], []), 0, x_hi[0] == 1
    for own_ref, came_ref, back_ref in pieces:
        groups, rows, _ = own_ref.shape
        came_scale, back_scale = scales(came_ref, groups), scales(back_ref, groups)
        half = rows // 2
        for g in range(groups):
            total = own_ref[g] + decode(came_ref, came_scale, g, g * rows, rows)
            total = total + decode(back_ref, back_scale, g, g * rows, rows)
            message, code = encode(total)
            first, second = message[:half].astype(jnp.int32), message[half:].astype(jnp.int32)
            near = slice(at, at + half)
            outs[2 * (g % 2)][near, :] = jnp.where(flip, second, first).astype(jnp.int16)
            outs[2 * (g % 2) + 1][near, :] = jnp.where(flip, first, second).astype(jnp.int16)
            codes[g % 2].append(code)
            at += half * (g % 2)
    for k in range(4):
        put_codes(outs[k], codes[k // 2])


def finish_kernel(pers, where, *refs):
    sums, out_ref = refs[:4], refs[-1]
    y, core = where[1], where[2]
    _, _, tiles, width2 = out_ref.shape
    width = width2 // 2
    groups = tiles * len(pers)
    scale = [scales(ref, groups) for ref in sums]
    start = base = 0
    for n, per in enumerate(pers):
        rows = 4 * per
        parts = []
        for b in range(2):
            stack = []
            for q in range(tiles):
                g, near = n * tiles + q, start + q * rows
                total = decode(sums[b], scale[b], g, near, rows) + decode(sums[2 + b], scale[2 + b], g, near, rows)
                stack.append(total)
            parts.append(jnp.swapaxes(jnp.stack(stack, axis=0), 0, 1))
        first = jnp.where(core == 0, parts[0], parts[1]).astype(out_ref.dtype)
        second = jnp.where(core == 0, parts[1], parts[0]).astype(out_ref.dtype)
        for to_y in range(4):
            slot = lax.rem(to_y - y + 4, 4)
            out_ref[slot, base : base + per, :, :width] = first[to_y * per : (to_y + 1) * per]
            out_ref[slot, base : base + per, :, width:] = second[to_y * per : (to_y + 1) * per]
        start += tiles * rows
        base += per


def place_kernel(count, where, *refs):
    parts, out_ref = refs[:count], refs[-1]
    base = 0
    for n in range(0, len(parts), 4):
        per = parts[n].shape[0]
        width = parts[n].shape[-1] // 2
        for a in range(4):
            from_y = lax.rem(where[1] - a + 4, 4)
            held = parts[n + a][...]
            for x in range(2):
                at = pl.ds(pl.multiple_of((x * 4 + from_y) * width, width), width)
                out_ref[base : base + per, :, at] = held[:, :, x * width : (x + 1) * width]
        base += per


LIMIT = 10 * 2**20


def stage(where, own, came):
    blocks, depth, half = own.shape
    return pl.pallas_call(
        stage_kernel,
        out_shape=pltpu.VMEM((blocks, depth, 2 * half), own.dtype),
        in_specs=[pl.BlockSpec(memory_space=pltpu.SMEM)] + [pl.BlockSpec(memory_space=pl.ANY)] * 2,
        out_specs=pl.BlockSpec(memory_space=pltpu.VMEM),
        scratch_shapes=[pltpu.SemaphoreType.DMA((2,))],
        compiler_params=pltpu.CompilerParams(vmem_limit_bytes=LIMIT),
        cost_estimate=pl.CostEstimate(flops=0, bytes_accessed=16 * 2**20, transcendentals=0),
        name="stage",
    )(where, pltpu.with_memory_space_constraint(own, pltpu.HBM), pltpu.with_memory_space_constraint(came, pltpu.HBM))


def partial(blk, prow, pos, gathered, staged):
    _, tiles, rows, depth = gathered[0].shape
    width = staged.shape[2]
    groups = 2 * tiles

    def whole(shape):
        return pl.BlockSpec(shape, lambda q, *_: (0,) * len(shape))

    message = jax.ShapeDtypeStruct((groups * rows + tail(groups), width), jnp.int16)
    kept = jax.ShapeDtypeStruct((groups, rows, width), jnp.float32)
    flops = 2 * 8 * rows * 4 * depth * width * tiles
    return pl.pallas_call(
        partial_kernel,
        grid_spec=pltpu.PrefetchScalarGridSpec(
            num_scalar_prefetch=3,
            grid=(tiles,),
            in_specs=[whole(a.shape) for a in gathered]
            + [pl.BlockSpec(memory_space=pltpu.VMEM)],
            out_specs=[whole(message.shape)] * 2 + [pl.BlockSpec((2, rows, width), lambda q, *_: (q, 0, 0))] * 2,
            scratch_shapes=[
                pltpu.VMEM((8, rows, width), jnp.float32),
                pltpu.VMEM((tail(groups), width), jnp.float32),
                pltpu.VMEM((tail(groups), width), jnp.float32),
            ],
        ),
        out_shape=[message, message, kept, kept],
        compiler_params=pltpu.CompilerParams(vmem_limit_bytes=LIMIT),
        cost_estimate=pl.CostEstimate(flops=flops, bytes_accessed=24 * 2**20, transcendentals=0),
        name="partial",
    )(blk, prow, pos, *gathered, pltpu.with_memory_space_constraint(staged, pltpu.VMEM))


def simple(kernel, outs, args, name, scalars=0):
    vmem = pl.BlockSpec(memory_space=pltpu.VMEM)
    smem = pl.BlockSpec(memory_space=pltpu.SMEM)
    return pl.pallas_call(
        kernel,
        out_shape=outs,
        in_specs=[smem] * scalars + [vmem] * (len(args) - scalars),
        out_specs=jax.tree.map(lambda _: vmem, outs),
        compiler_params=pltpu.CompilerParams(vmem_limit_bytes=LIMIT),
        cost_estimate=pl.CostEstimate(flops=2**22, bytes_accessed=2**22, transcendentals=0),
        name=name,
    )(*args)


def later(array, *others):
    return lax.optimization_barrier((array, *others))[0]


def on_device(amplitudes, integrals, blocks):
    _, tiles, depth = amplitudes.shape
    width = 2 * integrals.shape[2]
    row, col = lax.axis_index("row"), lax.axis_index("col")
    z, x_lo = row // 2, row % 2
    x_hi, y, core = col // 8, (col // 2) % 4, col % 2
    turn = 1 - 2 * core
    where = jnp.stack([x_hi, y, core]).astype(jnp.int32)

    number = jnp.arange(32, dtype=jnp.int32)
    key = blocks[:, 1] * 32 + number
    rank = jnp.sum((key[None, :] < key[:, None]).astype(jnp.int32), axis=1)
    hit = (rank[None, :] == number[:, None]).astype(jnp.int32)
    blk = jnp.sum(hit * number[None, :], axis=1)
    prow = jnp.sum(hit * blocks[:, 0][None, :], axis=1)

    slots = []
    for shift in (0, -turn, turn, 2):
        for flip in (0, 1):
            from_y = (y + shift + 4) % 4
            from_x = x_hi ^ flip
            to_z = 2 * from_x + from_y // 2
            ahead = ((to_z - z) * turn + 8) % 4
            slots.append(ahead * 2 + ((from_y % 2) ^ x_lo))
    pos = jnp.stack(slots).astype(jnp.int32)
    pos_first = jnp.stack(slots[0::2] + slots[1::2]).astype(jnp.int32)

    last = []

    def run(kernel, outs, args, name, scalars=0, after=()):
        args = list(args)
        args[scalars] = later(args[scalars], *last[-1:], *after)
        out = simple(kernel, outs, args, name, scalars)
        last.append(jax.tree.leaves(out)[0])
        return out

    shards = amplitudes.reshape(4, 2, 16, tiles, depth).transpose(3, 1, 0, 2, 4)
    own, at = [], 0
    for per in PIECES:
        own.append(shards[:, :, :, at : at + per].reshape(1, tiles, 8 * per, depth))
        at += per
    came = {1: move(own[1], X_HI)}
    v_other = move(integrals, CORE)
    gathered = {}

    def send(p, a0):
        gathered[p] = [a0, move(a0, Y_FORE), move(a0, Y_BACK), None]

    def forward(p):
        a1 = later(gathered[p][1], *last[-1:])
        gathered[p][3] = move(a1, Y_FORE)

    def fetch(members):
        rows = [8 * PIECES[p] for p in members]
        shape = jax.ShapeDtypeStruct((1, tiles, sum(rows), depth), jnp.bfloat16)
        block = jnp.concatenate([own[p] for p in members], axis=2)
        moved = move(run(copy_kernel, shape, (block,), "rest", after=(came[1],)), X_HI)
        at = 0
        for p, n in zip(members, rows):
            came[p] = moved[:, :, at : at + n]
            at += n

    def join(p):
        shape = jax.ShapeDtypeStruct((2, tiles, 8 * PIECES[p], depth), jnp.bfloat16)
        send(p, run(join_kernel, shape, (own[p], came[p]), "join", after=gathered[p - 1][1:3]))

    def turn_first():
        shape = jax.ShapeDtypeStruct((4, tiles, 8 * PIECES[0], depth), jnp.bfloat16)
        held = run(join_kernel, shape, tuple(gathered[0]), "join")
        gathered[0] = (held, move(held, X_HI))

    sums, ends, placed, staged = {}, {}, [], []

    def multiply(p):
        held = (later(gathered[p][0], last[-1]), *gathered[p][1:])
        far, back, kept, nxt = partial(blk, prow, pos if p else pos_first, held, staged[0])
        last.append(far)
        sums[p] = (kept, nxt, move(far, Z_FORE), move(back, Z_BACK))

    def relay(p):
        kept, nxt, far, back = sums[p]
        message = jax.ShapeDtypeStruct((16 * 8 * PIECES[p] + 16, width), jnp.int16)
        out = run(relay_kernel, message, (nxt, far), "relay", after=(back,))
        ends[p] = (kept, move(out, Z_FORE), back)

    def collect(members):
        groups = tiles * len(members)
        rows = tiles * 4 * sum(PIECES[p] for p in members)
        small = jax.ShapeDtypeStruct((rows + tail(groups), width), jnp.int16)
        args = [array for p in members for array in ends[p]]
        kernel = functools.partial(collect_kernel, len(members))
        out = run(kernel, [small] * 4, (where[:1], *args), "collect", scalars=1)
        return [move(m, t) for m, t in zip(out, X_SAME + X_OTHER)]

    def finish(members, out):
        pers = tuple(PIECES[p] for p in members)
        shape = jax.ShapeDtypeStruct((4, sum(pers), tiles, 2 * width), jnp.bfloat16)
        done = run(functools.partial(finish_kernel, pers), shape, (where, *out), "finish", scalars=1)
        placed.extend([done[0]] + [move(done[a], Y_SHIFT[a]) for a in range(1, 4)])

    send(0, own[0])
    forward(0)
    pending = {}
    for step in ORDER:
        name, p = step[0], step[1]
        if name == "join":
            join(p)
        elif name == "stage":
            staged.append(stage(later(where, last[-1]), integrals, v_other))
        elif name == "forward":
            forward(p)
        elif name == "fetch":
            fetch(p)
        elif name == "turn":
            turn_first()
        elif name == "multiply":
            multiply(p)
        elif name == "relay":
            relay(p)
        elif name == "collect":
            pending[p] = collect(p)
        else:
            finish(p, pending[p])
    return simple(
        functools.partial(place_kernel, len(placed)),
        jax.ShapeDtypeStruct((16, tiles, 8 * width), jnp.bfloat16),
        (where, *placed),
        "place",
        scalars=1,
    )


def solution(mesh):
    return jax.shard_map(
        on_device,
        mesh=mesh,
        in_specs=(P("col", None, "row"), P(None, "row", "col"), P()),
        out_specs=P(("row", "col"), None, None),
        check_vma=False,
    )
```
